256 devices in a mesh: cand: 128 (over x, z, y_lo, core), tok: 2 (over y_hi).
Axes of the slice: x: 4, y: 4 (y_hi: 2, y_lo: 2; y = y_hi * 2 + y_lo), z: 8, core: 2. Of those that a mesh axis runs over, the one named last changes fastest.
Arguments:
- embeddings: bfloat16 [128, 512, 1024], P('cand', 'tok')
- lengths: int32 [128], replicated, may hold values from 64 to 512, as said below
Outputs:
- utility: float32 [128, 24], P('cand')
The draws below stay inside these ranges and needn't reach their ends.
Inputs may be any that keep to these rules, and one draw needn't show every extreme that they name: The first lengths[c] token rows of candidate c are its tokens; the others are padding. Some candidate has all 512 slots valid.
All inputs are finite; a program needn't handle non-finite values.
Results may differ from the reference program's by a relative error of at most 0.0003.
Values may be sent and summed in bfloat16 or wider, within the bound.
No kernel may reach another device: no remote copies, remote signals or barrier semaphores. Data moves between devices by JAX's collectives and lax.ppermute only.
A program may use at most 64 MiB of HBM per device.

```python
import jax
import jax.numpy as jnp
from jax import lax

E = 1024
TOK = 512
CPD = 1
STEPS = 12
CANDS = 128
N_CAND = 128


def draw_embeddings(key, part):
    key = jax.random.fold_in(key, 1)
    keys = jax.random.split(key, 4)
    pool = jax.random.normal(keys[0], (256, E), jnp.float32)
    base = jax.random.randint(keys[1], (CANDS, 1), 0, 256)
    offsets = jax.random.randint(keys[2], (CANDS, TOK), 0, 96)
    concept = jnp.remainder(base + offsets, 256)
    vectors = pool[concept]
    noise = jax.random.normal(keys[3], (CANDS, TOK, E), jnp.float32)
    return (vectors + 0.7 * noise).astype(jnp.bfloat16)


def draw_lengths(key, part):
    key = jax.random.fold_in(key, 2)
    keys = jax.random.split(key, 2)
    counts = jax.random.randint(keys[0], (CANDS,), TOK // 8, TOK + 1)
    picked = jax.random.randint(keys[1], (), 0, CANDS)
    return counts.at[picked].set(TOK).astype(jnp.int32)


def setup_inputs(seed: int = 0) -> dict:
    splits = jax.random.split(jax.random.key(seed), 3)
    return {
        "embeddings": draw_embeddings(jax.random.fold_in(splits[2], 71), 0),
        "lengths": draw_lengths(jax.random.fold_in(splits[2], 71), 0),
    }


def normalize(emb):
    values = emb.astype(jnp.float32)
    factor = lax.rsqrt(lax.optimization_barrier(jnp.sum(values * values, axis=-1, keepdims=True)) + 1e-06)
    return (values * factor).astype(jnp.bfloat16)

def pair_scores(own, peer, own_len, peer_len):
    sims = jnp.einsum('ale,bme->ablm', own.astype(jnp.float32), peer.astype(jnp.float32))
    positions = jnp.arange(TOK, dtype=jnp.int32)
    own_valid = positions[None, :] < own_len[:, None]
    peer_valid = positions[None, :] < peer_len[:, None]
    rowbest = lax.optimization_barrier(jnp.max(jnp.where(peer_valid[None, :, None, :], sims, -3.0), axis=3))
    precision = lax.optimization_barrier(jnp.sum(jnp.where(own_valid[:, None, :], rowbest, 0.0), axis=2)) / own_len[:, None].astype(jnp.float32)
    colbest = lax.optimization_barrier(jnp.max(jnp.where(own_valid[:, None, :, None], sims, -3.0), axis=2))
    recall = lax.optimization_barrier(jnp.sum(jnp.where(peer_valid[None, :, :], colbest, 0.0), axis=2)) / peer_len[None, :].astype(jnp.float32)
    return 0.5 * (precision + recall)

def reference(embeddings, lengths):
    normed = normalize(embeddings)
    blocks = normed.reshape(N_CAND, CPD, TOK, E)
    len_blocks = lengths.reshape(N_CAND, CPD)

    def one_block(device):
        own = blocks[device]
        rows = []
        for offset in range(1, STEPS + 1):
            partner = (device + offset) % N_CAND
            rows.append(pair_scores(own, blocks[partner], len_blocks[device], len_blocks[partner]))
        return jnp.stack(rows)
    table = lax.map(one_block, jnp.arange(N_CAND, dtype=jnp.int32))
    forward = table.transpose(0, 2, 1, 3).reshape(CANDS, STEPS * CPD)
    rolled = jnp.stack([jnp.roll(table[:, index], index + 1, axis=0) for index in range(STEPS)], axis=1)
    backward = rolled.transpose(0, 3, 1, 2).reshape(CANDS, STEPS * CPD)
    return jnp.concatenate([forward, backward], axis=1)
```

```python
import functools

import jax
import jax.numpy as jnp
from jax import lax
from jax.experimental import pallas as pl
from jax.experimental.pallas import tpu as pltpu
from jax.sharding import PartitionSpec as P

STEPS = 12
AXES = ("cand", "tok")
GROUP = 4
REACH = STEPS // GROUP
LOW = -4.0
VMEM = 48 * 1024 * 1024


def place(flat):
    return flat // 8, (flat // 4) % 2, (flat // 2) % 2, flat % 2


def flat(group, y_lo, core, y_hi, groups):
    return (((group % groups) * 2 + y_lo) * 2 + core) * 2 + y_hi


def send(value, move):
    count = lax.axis_size(AXES)
    groups = count // 8
    pairs = [(i, flat(*move(*place(i)), groups)) for i in range(count)]
    return lax.ppermute(value, AXES, pairs)


def along(steps):
    return lambda g, l, c, h: (g + steps, l, c, h)


def within(dl, dc, dh):
    return lambda g, l, c, h: (g, l ^ dl, c ^ dc, h ^ dh)


def ring(g, l, c, h):
    y = (2 * h + l + (1 if c == 0 else -1)) % 4
    return (g, y % 2, c, y // 2)


def normalize_kernel(emb_ref, out_ref):
    values = emb_ref[0].astype(jnp.float32)
    factor = lax.rsqrt(jnp.sum(values * values, axis=-1, keepdims=True) + 1e-06)
    out_ref[...] = (values * factor).astype(jnp.bfloat16)


def normalize(emb):
    _, rows, width = emb.shape
    step = rows // 2
    return pl.pallas_call(
        normalize_kernel,
        grid=(rows // step,),
        in_specs=[pl.BlockSpec((1, step, width), lambda i: (0, i, 0))],
        out_specs=pl.BlockSpec((step, width), lambda i: (i, 0)),
        out_shape=jax.ShapeDtypeStruct((rows, width), jnp.bfloat16),
        name="normalize",
    )(emb)


def slot(ids, k, e):
    y_lo, core, y_hi = ids
    source = core ^ e
    y = (2 * y_hi + y_lo + jnp.where(source == 0, 4 - k, k)) % 4
    return 2 * (y % 2) + source, y // 2


def scan_kernel(n_x, n_a, dists, ids_ref, len_ref, *refs):
    xs, items = refs[:n_x], refs[n_x : n_x + n_a]
    msg_ref = refs[n_x + n_a]
    xbuf, abuf, racc, sems = refs[n_x + n_a + 1 :]
    group, y_lo, core, y_hi = (ids_ref[i] for i in range(4))
    cands = len_ref.shape[0]
    rows = xbuf.shape[0] // n_x
    copies = []
    for i, ref in enumerate(xs):
        copies.append(
            pltpu.make_async_copy(ref, xbuf.at[pl.ds(i * rows, rows)], sems.at[i])
        )
    for i, ref in enumerate(items):
        copies.append(pltpu.make_async_copy(ref, abuf.at[i], sems.at[n_x + i]))
    for copy in copies:
        copy.start()
    racc[...] = jnp.full(racc.shape, LOW, jnp.float32)
    lane = lax.broadcasted_iota(jnp.int32, (1, rows), 1)
    sub = lax.broadcasted_iota(jnp.int32, (rows, 1), 0)
    lane128 = lax.broadcasted_iota(jnp.int32, (1, 128), 1)
    own = 2 * y_lo + core
    x_valid = []
    for dist in dists:
        length = len_ref[(GROUP * (group + dist) + own) % cands]
        x_valid.append(length - rows * y_hi)
    for copy in copies[:n_x]:
        copy.wait()
    for a in range(n_a):
        copies[n_x + a].wait()

    @pl.loop(0, n_a)
    def _(a):
        cand, half = slot((y_lo, core, y_hi), a // 2, a % 2)
        a_valid = len_ref[GROUP * group + cand] - rows * half
        for i in range(n_x):
            sims = lax.dot_general(
                xbuf[i * rows : (i + 1) * rows, :],
                abuf[a],
                (((1,), (1,)), ((), ())),
                preferred_element_type=jnp.float32,
            )
            best = jnp.max(jnp.where(lane < a_valid, sims, LOW), axis=1, keepdims=True)
            racc[i] = jnp.where(lane128 == a, best, racc[i])
            col = jnp.max(jnp.where(sub < x_valid[i], sims, LOW), axis=0, keepdims=True)
            msg_ref[i, pl.ds(a, 1), :] = col

    for i in range(n_x):
        turned = racc[i].T
        paired = jnp.maximum(turned[0:4], turned[4:8])
        paired = jnp.where(lane < x_valid[i], paired, 0.0)
        msg_ref[i, 8:16, :] = jnp.concatenate([paired, jnp.zeros_like(paired)], axis=0)


def scan(ids, lengths, xs, dists, items):
    n_x, n_a = len(xs), len(items)
    rows, width = xs[0].shape
    flops = 2 * n_x * n_a * rows * rows * width
    return pl.pallas_call(
        functools.partial(scan_kernel, n_x, n_a, dists),
        in_specs=[pl.BlockSpec(memory_space=pltpu.SMEM)] * 2
        + [pl.BlockSpec(memory_space=pl.ANY)] * (n_x + n_a),
        out_specs=pl.BlockSpec(memory_space=pltpu.VMEM),
        out_shape=jax.ShapeDtypeStruct((n_x, 16, rows), jnp.float32),
        scratch_shapes=[
            pltpu.VMEM((n_x * rows, width), jnp.bfloat16),
            pltpu.VMEM((n_a, rows, width), jnp.bfloat16),
            pltpu.VMEM((n_x, rows, 128), jnp.float32),
            pltpu.SemaphoreType.DMA((n_x + n_a,)),
        ],
        compiler_params=pltpu.CompilerParams(vmem_limit_bytes=VMEM),
        cost_estimate=pl.CostEstimate(
            flops=flops, bytes_accessed=2 * (n_x + n_a) * rows * width, transcendentals=0
        ),
        name="scan",
    )(ids, lengths, *xs, *items)


def score_kernel(dists, ids_ref, len_ref, own_ref, got_ref, out_ref):
    group, y_lo, core, y_hi = (ids_ref[i] for i in range(4))
    cands = len_ref.shape[0]
    n_x, _, rows = own_ref.shape
    lane = lax.broadcasted_iota(jnp.int32, (8, rows), 1)
    sub = lax.broadcasted_iota(jnp.int32, (8, 1), 0)
    lane128 = lax.broadcasted_iota(jnp.int32, (8, 128), 1)
    valid = jnp.zeros((8, 1), jnp.int32)
    a_len = jnp.ones((8, 1), jnp.int32)
    for a in range(8):
        cand, half = slot((y_lo, core, y_hi), a // 2, a % 2)
        length = len_ref[GROUP * group + cand]
        valid = jnp.where(sub == a, length - rows * half, valid)
        a_len = jnp.where(sub == a, length, a_len)
    a_len = a_len.astype(jnp.float32)
    tile = jnp.zeros((8, 128), jnp.float32)
    for i, dist in enumerate(dists):
        x_len = len_ref[(GROUP * (group + dist) + 2 * y_lo + core) % cands]
        x_len = jnp.full((8, 1), x_len, jnp.int32).astype(jnp.float32)
        own, got = own_ref[i], got_ref[i]
        col = jnp.maximum(own[0:8], jnp.concatenate([got[4:8], got[0:4]], axis=0))
        col = jnp.sum(jnp.where(lane < valid, col, 0.0), axis=1, keepdims=True)
        recall = col + jnp.concatenate([col[4:8], col[0:4]], axis=0)
        precision = jnp.sum(own[8:16] + got[8:16], axis=1, keepdims=True)
        score = 0.5 * (precision / x_len + recall / a_len)
        tile = jnp.where(lane128 == dist, score, tile)
    out_ref[...] = tile


def score(ids, lengths, own, got, dists):
    return pl.pallas_call(
        functools.partial(score_kernel, dists),
        in_specs=[pl.BlockSpec(memory_space=pltpu.SMEM)] * 2
        + [pl.BlockSpec(memory_space=pltpu.VMEM)] * 2,
        out_specs=pl.BlockSpec(memory_space=pltpu.VMEM),
        out_shape=jax.ShapeDtypeStruct((8, 128), jnp.float32),
        name="score",
    )(ids, lengths, own, got)


def place_kernel(ids_ref, *refs):
    near, early, late = refs[0], refs[1:5], refs[5:9]
    back = refs[9:12]
    out_ref = refs[12]
    y_lo, core = ids_ref[1], ids_ref[2]
    own = 2 * y_lo + core
    sub = lax.broadcasted_iota(jnp.int32, (8, 128), 0)
    lane = lax.broadcasted_iota(jnp.int32, (8, 128), 1)
    other = 2 * (y_lo ^ (sub // 2)) + (core ^ (sub % 2))
    total = jnp.zeros((8, 128), jnp.float32)

    def add(total, values, steps, base, used):
        use = (steps >= 1) & (steps <= STEPS) & (lane == base + steps - 1) & (sub < 4) & used
        return total + jnp.where(use, values, 0.0)

    own_group = near[:, 0:1]
    total = add(total, own_group, other - own, 0, sub < 4)
    total = add(total, own_group, own - other, STEPS, sub < 4)
    for a in range(4):
        for dist in range(1, REACH + 1):
            tile = (early if dist < REACH else late)[a]
            total = add(total, tile[:, dist : dist + 1], GROUP * dist + other - own, 0, sub == a)
    for dist in range(1, REACH + 1):
        tile = back[dist - 1]
        total = add(
            total, tile[:, dist : dist + 1], GROUP * dist + own - other, STEPS, sub < 4
        )
    out_ref[...] = jnp.sum(total, axis=0, keepdims=True)[:, : 2 * STEPS]


def placed(ids, near, early, late, back):
    return pl.pallas_call(
        place_kernel,
        in_specs=[pl.BlockSpec(memory_space=pltpu.SMEM)]
        + [pl.BlockSpec(memory_space=pltpu.VMEM)] * 12,
        out_specs=pl.BlockSpec(memory_space=pltpu.VMEM),
        out_shape=jax.ShapeDtypeStruct((1, 2 * STEPS), jnp.float32),
        name="placed",
    )(ids, near, *early, *late, *back)


def on_device(embeddings, lengths):
    device = lax.axis_index("cand")
    ids = jnp.stack(
        [device // 4, (device // 2) % 2, device % 2, lax.axis_index("tok")]
    ).astype(jnp.int32)
    own = normalize(embeddings)
    peer = own
    peers = []
    for _ in range(REACH):
        peer = send(peer, along(-1))
        peers.append(peer)
    items = []
    piece = own
    for k in range(4):
        items += [piece, send(piece, within(0, 1, 0))]
        if k < 3:
            piece = send(piece, ring)
    first = scan(ids, lengths, [own, *peers[:-1]], tuple(range(REACH)), items)
    got = send(first, within(0, 0, 1))
    tile = score(ids, lengths, first, got, tuple(range(REACH)))
    early = [tile] + [send(tile, within(a // 2, a % 2, 0)) for a in range(1, 4)]
    back = [send(tile, along(dist)) for dist in range(1, REACH)]
    last = scan(ids, lengths, [peers[-1]], (REACH,), items)
    got = send(last, within(0, 0, 1))
    tile3 = score(ids, lengths, last, got, (REACH,))
    late = [tile3] + [send(tile3, within(a // 2, a % 2, 0)) for a in range(1, 4)]
    back.append(send(tile3, along(REACH)))
    return placed(ids, tile, early, late, back)


def solution(mesh):
    in_specs = (P("cand", "tok", None), P())
    out_specs = P("cand", None)
    return jax.shard_map(
        on_device, mesh=mesh, in_specs=in_specs, out_specs=out_specs, check_vma=False
    )
```

```python
import functools

import jax
import jax.numpy as jnp
from jax import lax
from jax.experimental import pallas as pl
from jax.experimental.pallas import tpu as pltpu
from jax.sharding import PartitionSpec as P

STEPS = 12
AXES = ("cand", "tok")
GROUP = 4
LOW = -4.0
VMEM = 48 * 1024 * 1024
IN_VMEM = pl.BlockSpec(memory_space=pltpu.VMEM)
IN_SMEM = pl.BlockSpec(memory_space=pltpu.SMEM)
X_VALID, X_LEN, A_VALID, A_LEN, Y_LO, CORE = 0, 1, 8, 16, 24, 25


def place(flat):
    return flat // 8, (flat // 4) % 2, (flat // 2) % 2, flat % 2


def flat(group, y_lo, core, y_hi, groups):
    return (((group % groups) * 2 + y_lo) * 2 + core) * 2 + y_hi


def send(value, move):
    count = lax.axis_size(AXES)
    groups = count // 8
    pairs = [(i, flat(*move(*place(i)), groups)) for i in range(count)]
    return lax.ppermute(value, AXES, pairs)


def shift(dg=0, dl=0, dc=0, dh=0):
    return lambda g, l, c, h: (g + dg, l ^ dl, c ^ dc, h ^ dh)


def ring(way):
    def move(g, l, c, h):
        y = (2 * h + l + (way if c == 0 else -way)) % 4
        return (g, y % 2, c, y // 2)

    return move


def normalize_kernel(emb_ref, out_ref):
    values = emb_ref[0].astype(jnp.float32)
    factor = lax.rsqrt(jnp.sum(values * values, axis=-1, keepdims=True) + 1e-06)
    out_ref[...] = (values * factor).astype(jnp.bfloat16)


def normalize(emb):
    _, rows, width = emb.shape
    step = rows // 2
    return pl.pallas_call(
        normalize_kernel,
        grid=(rows // step,),
        in_specs=[pl.BlockSpec((1, step, width), lambda i: (0, i, 0))],
        out_specs=pl.BlockSpec((step, width), lambda i: (i, 0)),
        out_shape=jax.ShapeDtypeStruct((rows, width), jnp.bfloat16),
        name="normalize",
    )(emb)


def plan_kernel(rows, ids_ref, len_ref, par_ref):
    group, y_lo, core, y_hi = (ids_ref[i] for i in range(4))
    cands = len_ref.shape[0]
    sub = lax.broadcasted_iota(jnp.int32, (8, 128), 0)
    lane = lax.broadcasted_iota(jnp.int32, (8, 128), 1)
    for f in range(2):
        side = core ^ f
        tile = jnp.zeros((8, 128), jnp.int32)
        for x in range(8):
            cand = GROUP * (group + 1 - x // 2) + 2 * y_lo + (side ^ (x % 2))
            length = len_ref[(cand + cands) % cands]
            tile = jnp.where((sub == x) & (lane == X_VALID), length - rows * y_hi, tile)
            tile = jnp.where((sub == x) & (lane == X_LEN), length, tile)
        for k in range(4):
            y = (2 * y_hi + y_lo + jnp.where(side == 0, 4 - k, k)) % 4
            length = len_ref[(GROUP * (group + 1) + 2 * (y % 2) + side) % cands]
            tile = jnp.where(lane == A_VALID + k, length - rows * (y // 2), tile)
            if k < 2:
                tile = jnp.where(lane == A_LEN + k, length, tile)
        tile = jnp.where(lane == Y_LO, y_lo, tile)
        tile = jnp.where(lane == CORE, side, tile)
        par_ref[8 * f : 8 * f + 8] = tile


def plan(ids, lengths, rows):
    return pl.pallas_call(
        functools.partial(plan_kernel, rows),
        in_specs=[IN_SMEM] * 2,
        out_specs=IN_VMEM,
        out_shape=jax.ShapeDtypeStruct((16, 128), jnp.int32),
        name="plan",
    )(ids, lengths)


def scan_kernel(x_ids, ks, first, last, *refs):
    n_x, n_a = len(x_ids), len(ks)
    par_ref, refs = refs[0], refs[1:]
    xs, refs = refs[:n_x], refs[n_x:]
    items, refs = refs[:n_a], refs[n_a:]
    if first:
        row_out, col_out = refs[:2]
        row_out[...] = jnp.full(row_out.shape, LOW, jnp.float32)
        col_out[...] = jnp.full(col_out.shape, LOW, jnp.float32)
        rest = refs[2:]
    else:
        row_in, col_in, row_out, col_out = refs[:4]
        row_out[...] = row_in[...]
        col_out[...] = col_in[...]
        rest = refs[4:]
    rows = xs[0].shape[0]
    lane = lax.broadcasted_iota(jnp.int32, (1, rows), 1)
    sub = lax.broadcasted_iota(jnp.int32, (rows, 1), 0)
    lane128 = lax.broadcasted_iota(jnp.int32, (1, 128), 1)
    for i, x in enumerate(x_ids):
        x_mask = sub < par_ref[x : x + 1, X_VALID : X_VALID + 1]
        for j, k in enumerate(ks):
            a_mask = lane < par_ref[0:1, A_VALID + k : A_VALID + k + 1]
            sims = lax.dot_general(
                xs[i][...],
                items[j][...],
                (((1,), (1,)), ((), ())),
                preferred_element_type=jnp.float32,
            )
            best = jnp.max(jnp.where(a_mask, sims, LOW), axis=1, keepdims=True)
            row_out[...] = jnp.where(lane128 == 8 * k + x, best, row_out[...])
            col = jnp.max(jnp.where(x_mask, sims, LOW), axis=0, keepdims=True)
            col_out[k, x : x + 1, :] = col
    if last:
        turned = row_out[...].T
        lanes = lax.broadcasted_iota(jnp.int32, (8, rows), 1)
        valid = lanes < par_ref[0:8, X_VALID : X_VALID + 1]
        sums = jnp.zeros((8, rows), jnp.float32)
        for p in range(2):
            best = jnp.maximum(turned[8 * p : 8 * p + 8], turned[8 * p + 16 : 8 * p + 24])
            total = jnp.sum(jnp.where(valid, best, 0.0), axis=1, keepdims=True)
            sums = jnp.where(lanes == p, total, sums)
        col_out[4] = sums


def scan(par, xs, x_ids, items, ks, state=None, last=False):
    n_x, n_a = len(xs), len(items)
    rows, width = xs[0].shape
    state = [] if state is None else list(state)
    return pl.pallas_call(
        functools.partial(scan_kernel, x_ids, ks, not state, last),
        in_specs=[IN_VMEM] * (1 + n_x + n_a + len(state)),
        out_specs=[IN_VMEM] * 2,
        out_shape=[
            jax.ShapeDtypeStruct((rows, 128), jnp.float32),
            jax.ShapeDtypeStruct((5, 8, rows), jnp.float32),
        ],
        compiler_params=pltpu.CompilerParams(vmem_limit_bytes=VMEM),
        cost_estimate=pl.CostEstimate(
            flops=2 * n_x * n_a * rows * rows * width,
            bytes_accessed=2 * (n_x + n_a) * rows * width,
            transcendentals=0,
        ),
        name="scan",
    )(par, *xs, *items, *state)


def score_kernel(par_ref, own_ref, over_ref, core_ref, both_ref, out_ref):
    rows = own_ref.shape[2]
    lane = lax.broadcasted_iota(jnp.int32, (8, rows), 1)
    lane128 = lax.broadcasted_iota(jnp.int32, (8, 128), 1)
    par = par_ref[...]

    def scores(par, one, two):
        x_len = par[:, X_LEN : X_LEN + 1].astype(jnp.float32)
        sums = []
        for k in range(4):
            col = jnp.maximum(one[k], two[k ^ 2])
            valid = lane < par[:, A_VALID + k : A_VALID + k + 1]
            sums.append(jnp.sum(jnp.where(valid, col, 0.0), axis=1, keepdims=True))
        precision = one[4][:, :2] + two[4][:, :2]
        tile = jnp.zeros((8, 128), jnp.float32)
        for p in range(2):
            a_len = par[:, A_LEN + p : A_LEN + p + 1].astype(jnp.float32)
            recall = (sums[p] + sums[p + 2]) / a_len
            tile = jnp.where(
                lane128 == p, 0.5 * (precision[:, p : p + 1] / x_len + recall), tile
            )
        return tile

    out_ref[0:8] = scores(par[0:8], own_ref, over_ref)
    out_ref[8:16] = scores(par[8:16], core_ref, both_ref)


def score(par, own, over, core, both):
    return pl.pallas_call(
        score_kernel,
        in_specs=[IN_VMEM] * 5,
        out_specs=IN_VMEM,
        out_shape=jax.ShapeDtypeStruct((16, 128), jnp.float32),
        name="score",
    )(par, own, over, core, both)


def put_kernel(par_ref, own_ref, same_ref, other_ref, one_ref, two_ref, out_ref):
    y_lo, core = par_ref[0:1, Y_LO : Y_LO + 1], par_ref[0:1, CORE : CORE + 1]
    sub = lax.broadcasted_iota(jnp.int32, (16, 128), 0)
    lane = lax.broadcasted_iota(jnp.int32, (16, 128), 1)
    f, d, e = sub // 8, (sub % 8) // 2, sub % 2
    own = 2 * y_lo + core
    total = jnp.zeros((16, 128), jnp.float32)

    def add(total, values, steps, base, used):
        use = used & (steps >= 1) & (steps <= STEPS) & (lane == base + steps - 1)
        return total + jnp.where(use, values, 0.0)

    for p, ref in enumerate((same_ref, other_ref)):
        values = ref[:, p : p + 1]
        x = 2 * (y_lo ^ p) + (core ^ e)
        steps = GROUP * d + own - x
        total = add(total, values, steps, STEPS, f == 0)
        total = add(total, values, -steps, 0, (f == 0) & (d == 0))
    for dist, ref in enumerate((own_ref, one_ref, two_ref), 1):
        for p in range(2):
            values = ref[:, p : p + 1]
            a = 2 * (y_lo ^ p) + (core ^ f)
            total = add(total, values, GROUP * dist + a - own, 0, (d == dist) & (e == f))
    out_ref[...] = jnp.sum(total, axis=0, keepdims=True)[:, : 2 * STEPS]


def put(par, own, same, other, one, two):
    return pl.pallas_call(
        put_kernel,
        in_specs=[IN_VMEM] * 6,
        out_specs=IN_VMEM,
        out_shape=jax.ShapeDtypeStruct((1, 2 * STEPS), jnp.float32),
        name="put",
    )(par, own, same, other, one, two)


def on_device(embeddings, lengths):
    device = lax.axis_index("cand")
    rows = embeddings.shape[1]
    ids = jnp.stack(
        [device // 4, (device // 2) % 2, device % 2, lax.axis_index("tok")]
    ).astype(jnp.int32)
    par = plan(ids, lengths, rows)
    own = normalize(embeddings)

    right = send(own, shift(dg=-1))
    left = send(own, shift(dg=1))
    over = send(own, shift(dh=1))
    own_c = send(own, shift(dc=1))
    right, left, over, own_c = lax.optimization_barrier((right, left, over, own_c))

    item1 = send(right, ring(1))
    item3 = send(right, ring(-1))
    item2 = send(over, shift(dg=-1))
    far = send(left, shift(dg=1))
    right_c = send(right, shift(dc=1))
    left_c = send(left, shift(dc=1))
    near = [right, right_c, own, own_c, left, left_c]
    state = scan(par, near, range(6), [right], [0])
    item1, item2, item3, far = lax.optimization_barrier((item1, item2, item3, far))
    far_c = send(far, shift(dc=1))
    state = scan(par, near, range(6), [item1, item2, item3], [1, 2, 3], state)
    _, message = scan(
        par, [far, far_c], [6, 7], [right, item1, item2, item3], range(4), state, True
    )

    over = send(message, shift(dh=1))
    core = send(message, shift(dc=1))
    both = send(message, shift(dc=1, dh=1))
    tile = score(par, message, over, core, both)
    same = send(tile, shift(dg=1))
    other = send(tile, shift(dg=1, dl=1))
    one = send(tile, shift(dg=-1))
    two = send(tile, shift(dg=-2))
    return put(par, tile, same, other, one, two)


def solution(mesh):
    in_specs = (P("cand", "tok", None), P())
    out_specs = P("cand", None)
    return jax.shard_map(
        on_device, mesh=mesh, in_specs=in_specs, out_specs=out_specs, check_vma=False
    )
```

```python
import functools

import jax
import jax.numpy as jnp
from jax import lax
from jax.experimental import pallas as pl
from jax.experimental.pallas import tpu as pltpu
from jax.sharding import PartitionSpec as P

STEPS = 12
AXES = ("cand", "tok")
GROUP = 4
LOW = -4.0
SMALL = pltpu.CompilerParams(vmem_limit_bytes=4 * 1024 * 1024)
LARGE = pltpu.CompilerParams(vmem_limit_bytes=8 * 1024 * 1024)
IN_VMEM = pl.BlockSpec(memory_space=pltpu.VMEM)
IN_SMEM = pl.BlockSpec(memory_space=pltpu.SMEM)
X_VALID, X_LEN, A_VALID, A_LEN, Y_LO, CORE = 0, 1, 8, 16, 24, 25


def place(flat):
    return flat // 8, (flat // 4) % 2, (flat // 2) % 2, flat % 2


def flat(group, y_lo, core, y_hi, groups):
    return (((group % groups) * 2 + y_lo) * 2 + core) * 2 + y_hi


def send(value, move):
    count = lax.axis_size(AXES)
    groups = count // 8
    pairs = [(i, flat(*move(*place(i)), groups)) for i in range(count)]
    return lax.ppermute(value, AXES, pairs)


def shift(dg=0, dl=0, dc=0, dh=0):
    return lambda g, l, c, h: (g + dg, l ^ dl, c ^ dc, h ^ dh)


def ring(way):
    def move(g, l, c, h):
        y = (2 * h + l + (way if c == 0 else -way)) % 4
        return (g, y % 2, c, y // 2)

    return move


PARTS = 8


def normalize_kernel(emb_ref, out_ref, buf, sems):
    step = out_ref.shape[0] // PARTS
    copies = [
        pltpu.make_async_copy(
            emb_ref.at[0, pl.ds(i * step, step)], buf.at[i], sems.at[i]
        )
        for i in range(PARTS)
    ]
    for copy in copies:
        copy.start()
    for i, copy in enumerate(copies):
        copy.wait()
        values = buf[i].astype(jnp.float32)
        factor = lax.rsqrt(jnp.sum(values * values, axis=-1, keepdims=True) + 1e-06)
        out_ref[i * step : (i + 1) * step, :] = (values * factor).astype(jnp.bfloat16)


def normalize(emb):
    _, rows, width = emb.shape
    return pl.pallas_call(
        normalize_kernel,
        in_specs=[pl.BlockSpec(memory_space=pl.ANY)],
        out_specs=IN_VMEM,
        out_shape=jax.ShapeDtypeStruct((rows, width), jnp.bfloat16),
        scratch_shapes=[
            pltpu.VMEM((PARTS, rows // PARTS, width), jnp.bfloat16),
            pltpu.SemaphoreType.DMA((PARTS,)),
        ],
        compiler_params=SMALL,
        name="normalize",
    )(emb)


def plan_kernel(rows, ids_ref, len_ref, par_ref):
    group, y_lo, core, y_hi = (ids_ref[i] for i in range(4))
    cands = len_ref.shape[0]
    sub = lax.broadcasted_iota(jnp.int32, (8, 128), 0)
    lane = lax.broadcasted_iota(jnp.int32, (8, 128), 1)
    for f in range(2):
        side = core ^ f
        tile = jnp.zeros((8, 128), jnp.int32)
        for x in range(8):
            cand = GROUP * (group + 1 - x // 2) + 2 * y_lo + (side ^ (x % 2))
            length = len_ref[(cand + cands) % cands]
            tile = jnp.where((sub == x) & (lane == X_VALID), length - rows * y_hi, tile)
            tile = jnp.where((sub == x) & (lane == X_LEN), length, tile)
        for k in range(4):
            y = (2 * y_hi + y_lo + jnp.where(side == 0, 4 - k, k)) % 4
            length = len_ref[(GROUP * (group + 1) + 2 * (y % 2) + side) % cands]
            tile = jnp.where(lane == A_VALID + k, length - rows * (y // 2), tile)
            if k < 2:
                tile = jnp.where(lane == A_LEN + k, length, tile)
        tile = jnp.where(lane == Y_LO, y_lo, tile)
        tile = jnp.where(lane == CORE, side, tile)
        par_ref[8 * f : 8 * f + 8] = tile
        if f == 0:
            turned = jnp.zeros((8, 128), jnp.int32)
            for x in range(8):
                cand = GROUP * (group + 1 - x // 2) + 2 * y_lo + (core ^ (x % 2))
                length = len_ref[(cand + cands) % cands]
                turned = jnp.where(lane % 8 == x, length - rows * y_hi, turned)
            par_ref[16:24] = turned


def plan(ids, lengths, rows):
    return pl.pallas_call(
        functools.partial(plan_kernel, rows),
        in_specs=[IN_SMEM] * 2,
        out_specs=IN_VMEM,
        out_shape=jax.ShapeDtypeStruct((24, 128), jnp.int32),
        compiler_params=SMALL,
        name="plan",
    )(ids, lengths)


def scan_kernel(x_ids, ks, first, last, *refs):
    n_x, n_a = len(x_ids), len(ks)
    par_ref, refs = refs[0], refs[1:]
    xs, refs = refs[:n_x], refs[n_x:]
    items, refs = refs[:n_a], refs[n_a:]
    if first:
        row_out, col_out = refs[:2]
        row_out[...] = jnp.full(row_out.shape, LOW, jnp.float32)
        col_out[...] = jnp.full(col_out.shape, LOW, jnp.float32)
        rest = refs[2:]
    else:
        row_in, col_in, row_out, col_out = refs[:4]
        row_out[...] = row_in[...]
        col_out[...] = col_in[...]
        rest = refs[4:]
    rows = xs[0].shape[0]
    lane = lax.broadcasted_iota(jnp.int32, (1, rows), 1)
    sub = lax.broadcasted_iota(jnp.int32, (rows, 1), 0)
    lane128 = lax.broadcasted_iota(jnp.int32, (1, 128), 1)
    for i, x in enumerate(x_ids):
        x_mask = sub < par_ref[x : x + 1, X_VALID : X_VALID + 1]
        for j, k in enumerate(ks):
            a_mask = lane < par_ref[0:1, A_VALID + k : A_VALID + k + 1]
            sims = lax.dot_general(
                xs[i][...],
                items[j][...],
                (((1,), (1,)), ((), ())),
                preferred_element_type=jnp.float32,
            )
            best = jnp.max(jnp.where(a_mask, sims, LOW), axis=1, keepdims=True)
            row_out[...] = jnp.where(lane128 == 8 * k + x, best, row_out[...])
            col = jnp.max(jnp.where(x_mask, sims, LOW), axis=0, keepdims=True)
            col_out[k, x : x + 1, :] = col
    if last:
        best = row_out[...]
        best = jnp.maximum(best, pltpu.roll(best, 128 - 16, 1))
        total = jnp.where(sub < par_ref[16:17, :], best, 0.0)
        total = jnp.sum(total, axis=0, keepdims=True)
        col_out[4, :, 0:128] = jnp.broadcast_to(total, (8, 128))
        col_out[4, :, 128:256] = jnp.zeros((8, 128), jnp.float32)


def scan(par, xs, x_ids, items, ks, state=None, last=False):
    n_x, n_a = len(xs), len(items)
    rows, width = xs[0].shape
    state = [] if state is None else list(state)
    return pl.pallas_call(
        functools.partial(scan_kernel, x_ids, ks, not state, last),
        in_specs=[IN_VMEM] * (1 + n_x + n_a + len(state)),
        out_specs=[IN_VMEM] * 2,
        out_shape=[
            jax.ShapeDtypeStruct((rows, 128), jnp.float32),
            jax.ShapeDtypeStruct((5, 8, rows), jnp.float32),
        ],
        compiler_params=LARGE,
        cost_estimate=pl.CostEstimate(
            flops=2 * n_x * n_a * rows * rows * width,
            bytes_accessed=2 * (n_x + n_a) * rows * width,
            transcendentals=0,
        ),
        name="scan",
    )(par, *xs, *items, *state)


def score_kernel(par_ref, own_ref, over_ref, core_ref, both_ref, out_ref):
    rows = own_ref.shape[2]
    lane = lax.broadcasted_iota(jnp.int32, (8, rows), 1)
    lane128 = lax.broadcasted_iota(jnp.int32, (8, 128), 1)
    sub128 = lax.broadcasted_iota(jnp.int32, (8, 128), 0)
    par = par_ref[...]

    def scores(par, one, two):
        x_len = par[:, X_LEN : X_LEN + 1].astype(jnp.float32)
        sums = []
        for k in range(4):
            col = jnp.maximum(one[k], two[k ^ 2])
            valid = lane < par[:, A_VALID + k : A_VALID + k + 1]
            sums.append(jnp.sum(jnp.where(valid, col, 0.0), axis=1, keepdims=True))
        precision = one[4][:, :128] + two[4][:, :128]
        tile = jnp.zeros((8, 128), jnp.float32)
        for p in range(2):
            a_len = par[:, A_LEN + p : A_LEN + p + 1].astype(jnp.float32)
            recall = (sums[p] + sums[p + 2]) / a_len
            mine = jnp.where(lane128 == 8 * p + sub128, precision, 0.0)
            mine = jnp.sum(mine, axis=1, keepdims=True) / x_len
            tile = jnp.where(lane128 == p, 0.5 * (mine + recall), tile)
        return tile

    out_ref[0:8] = scores(par[0:8], own_ref, over_ref)
    out_ref[8:16] = scores(par[8:16], core_ref, both_ref)


def score(par, own, over, core, both):
    return pl.pallas_call(
        score_kernel,
        in_specs=[IN_VMEM] * 5,
        out_specs=IN_VMEM,
        out_shape=jax.ShapeDtypeStruct((16, 128), jnp.float32),
        compiler_params=SMALL,
        name="score",
    )(par, own, over, core, both)


def put_kernel(par_ref, own_ref, same_ref, other_ref, one_ref, two_ref, out_ref):
    y_lo, core = par_ref[0:1, Y_LO : Y_LO + 1], par_ref[0:1, CORE : CORE + 1]
    sub = lax.broadcasted_iota(jnp.int32, (16, 128), 0)
    lane = lax.broadcasted_iota(jnp.int32, (16, 128), 1)
    f, d, e = sub // 8, (sub % 8) // 2, sub % 2
    own = 2 * y_lo + core
    total = jnp.zeros((16, 128), jnp.float32)

    def add(total, values, steps, base, used):
        use = used & (steps >= 1) & (steps <= STEPS) & (lane == base + steps - 1)
        return total + jnp.where(use, values, 0.0)

    for p, ref in enumerate((same_ref, other_ref)):
        values = ref[:, p : p + 1]
        x = 2 * (y_lo ^ p) + (core ^ e)
        steps = GROUP * d + own - x
        total = add(total, values, steps, STEPS, f == 0)
        total = add(total, values, -steps, 0, (f == 0) & (d == 0))
    for dist, ref in enumerate((own_ref, one_ref, two_ref), 1):
        for p in range(2):
            values = ref[:, p : p + 1]
            a = 2 * (y_lo ^ p) + (core ^ f)
            total = add(total, values, GROUP * dist + a - own, 0, (d == dist) & (e == f))
    out_ref[...] = jnp.sum(total, axis=0, keepdims=True)[:, : 2 * STEPS]


def put(par, own, same, other, one, two):
    return pl.pallas_call(
        put_kernel,
        in_specs=[IN_VMEM] * 6,
        out_specs=IN_VMEM,
        out_shape=jax.ShapeDtypeStruct((1, 2 * STEPS), jnp.float32),
        compiler_params=SMALL,
        name="put",
    )(par, own, same, other, one, two)


def on_device(embeddings, lengths):
    device = lax.axis_index("cand")
    rows = embeddings.shape[1]
    ids = jnp.stack(
        [device // 4, (device // 2) % 2, device % 2, lax.axis_index("tok")]
    ).astype(jnp.int32)
    par = plan(ids, lengths, rows)
    own = normalize(embeddings)

    own_c = send(own, shift(dc=1))
    right = send(own, shift(dg=-1))
    left = send(own, shift(dg=1))
    over = send(own, shift(dh=1))
    own_c, right, left, over, par = lax.optimization_barrier(
        (own_c, right, left, over, par)
    )

    right_c = send(right, shift(dc=1))
    left_c = send(left, shift(dc=1))
    item3 = send(right, ring(-1))
    item1 = send(right, ring(1))
    item2 = send(over, shift(dg=-1))
    far = send(left, shift(dg=1))
    near = [right, right_c, own, own_c, left, left_c]
    state = scan(par, near, range(6), [right], [0])
    item1, item2, item3, far = lax.optimization_barrier((item1, item2, item3, far))
    far_c = send(far, shift(dc=1))
    state = scan(par, near, range(6), [item1, item2, item3], [1, 2, 3], state)
    _, message = scan(
        par, [far, far_c], [6, 7], [right, item1, item2, item3], range(4), state, True
    )

    over = send(message, shift(dh=1))
    core = send(message, shift(dc=1))
    both = send(message, shift(dc=1, dh=1))
    tile = score(par, message, over, core, both)
    same = send(tile, shift(dg=1))
    other = send(tile, shift(dg=1, dl=1))
    one = send(tile, shift(dg=-1))
    two = send(tile, shift(dg=-2))
    return put(par, tile, same, other, one, two)


def solution(mesh):
    in_specs = (P("cand", "tok", None), P())
    out_specs = P("cand", None)
    return jax.shard_map(
        on_device, mesh=mesh, in_specs=in_specs, out_specs=out_specs, check_vma=False
    )
```

```python
import functools

import jax
import jax.numpy as jnp
from jax import lax
from jax.experimental import pallas as pl
from jax.experimental.pallas import tpu as pltpu
from jax.sharding import PartitionSpec as P

STEPS = 12
WIDE = 64
AXES = ("cand", "tok")
GROUP = 4
LOW = -4.0
SMALL = pltpu.CompilerParams(vmem_limit_bytes=4 * 1024 * 1024)
LARGE = pltpu.CompilerParams(vmem_limit_bytes=8 * 1024 * 1024)
IN_VMEM = pl.BlockSpec(memory_space=pltpu.VMEM)
IN_SMEM = pl.BlockSpec(memory_space=pltpu.SMEM)
X_VALID, X_LEN, A_VALID, A_LEN, Y_LO, CORE = 0, 1, 8, 16, 24, 25


def place(flat):
    return flat // 8, (flat // 4) % 2, (flat // 2) % 2, flat % 2


def flat(group, y_lo, core, y_hi, groups):
    return (((group % groups) * 2 + y_lo) * 2 + core) * 2 + y_hi


def send(value, move):
    count = lax.axis_size(AXES)
    groups = count // 8
    pairs = [(i, flat(*move(*place(i)), groups)) for i in range(count)]
    return lax.ppermute(value, AXES, pairs)


def shift(dg=0, dl=0, dc=0, dh=0):
    return lambda g, l, c, h: (g + dg, l ^ dl, c ^ dc, h ^ dh)


def ring(way):
    def move(g, l, c, h):
        y = (2 * h + l + (way if c == 0 else -way)) % 4
        return (g, y % 2, c, y // 2)

    return move


PARTS = 4


def normalize_kernel(emb_ref, out_ref):
    step = out_ref.shape[0] // PARTS
    for i in range(PARTS):
        values = emb_ref[0, i * step : (i + 1) * step, :].astype(jnp.float32)
        factor = lax.rsqrt(jnp.sum(values * values, axis=-1, keepdims=True) + 1e-06)
        out_ref[i * step : (i + 1) * step, :] = (values * factor).astype(jnp.bfloat16)


def normalize(emb):
    _, rows, width = emb.shape
    return pl.pallas_call(
        normalize_kernel,
        in_specs=[IN_VMEM],
        out_specs=IN_VMEM,
        out_shape=jax.ShapeDtypeStruct((rows, width), jnp.bfloat16),
        compiler_params=SMALL,
        name="normalize",
    )(emb)


def plan_kernel(rows, ids_ref, len_ref, par_ref):
    group, y_lo, core, y_hi = (ids_ref[i] for i in range(4))
    cands = len_ref.shape[0]
    sub = lax.broadcasted_iota(jnp.int32, (8, 128), 0)
    lane = lax.broadcasted_iota(jnp.int32, (8, 128), 1)
    for f in range(2):
        side = core ^ f
        tile = jnp.zeros((8, 128), jnp.int32)
        for x in range(8):
            cand = GROUP * (group + 1 - x // 2) + 2 * y_lo + (side ^ (x % 2))
            length = len_ref[(cand + cands) % cands]
            tile = jnp.where((sub == x) & (lane == X_VALID), length - rows * y_hi, tile)
            tile = jnp.where((sub == x) & (lane == X_LEN), length, tile)
        for k in range(4):
            y = (2 * y_hi + y_lo + jnp.where(side == 0, 4 - k, k)) % 4
            length = len_ref[(GROUP * (group + 1) + 2 * (y % 2) + side) % cands]
            tile = jnp.where(lane == A_VALID + k, length - rows * (y // 2), tile)
            if k < 2:
                tile = jnp.where(lane == A_LEN + k, length, tile)
        tile = jnp.where(lane == Y_LO, y_lo, tile)
        tile = jnp.where(lane == CORE, side, tile)
        par_ref[8 * f : 8 * f + 8] = tile
        if f == 0:
            turned = jnp.zeros((8, 128), jnp.int32)
            for x in range(8):
                cand = GROUP * (group + 1 - x // 2) + 2 * y_lo + (core ^ (x % 2))
                length = len_ref[(cand + cands) % cands]
                turned = jnp.where(lane % 8 == x, length - rows * y_hi, turned)
            par_ref[16:24] = turned


def plan(ids, lengths, rows):
    return pl.pallas_call(
        functools.partial(plan_kernel, rows),
        in_specs=[IN_SMEM] * 2,
        out_specs=IN_VMEM,
        out_shape=jax.ShapeDtypeStruct((24, 128), jnp.int32),
        compiler_params=SMALL,
        name="plan",
    )(ids, lengths)


def scan_kernel(par_ref, *refs):
    xs, items, out_ref, best_ref = refs[:8], refs[8:12], refs[12], refs[13]
    rows = xs[0].shape[0]
    lane = lax.broadcasted_iota(jnp.int32, (1, rows), 1)
    sub = lax.broadcasted_iota(jnp.int32, (rows, 1), 0)
    lane128 = lax.broadcasted_iota(jnp.int32, (1, 128), 1)
    best_ref[...] = jnp.full(best_ref.shape, LOW, jnp.float32)
    for k in (0, 1, 3, 2):
        a_mask = lane < par_ref[0:1, A_VALID + k : A_VALID + k + 1]
        for x in range(8):
            if x == 0 and k % 2 == 0:
                out_ref[k, x : x + 1, :] = jnp.full((1, rows), LOW, jnp.float32)
                continue
            x_mask = sub < par_ref[x : x + 1, X_VALID : X_VALID + 1]
            at = slice(rows, 2 * rows) if x == 1 else slice(0, rows)
            sims = lax.dot_general(
                xs[x][at, :],
                items[k][...],
                (((1,), (1,)), ((), ())),
                preferred_element_type=jnp.float32,
            )
            best = jnp.max(jnp.where(a_mask, sims, LOW), axis=1, keepdims=True)
            best_ref[...] = jnp.where(lane128 == 8 * k + x, best, best_ref[...])
            col = jnp.max(jnp.where(x_mask, sims, LOW), axis=0, keepdims=True)
            out_ref[k, x : x + 1, :] = col
    best = best_ref[...]
    best = jnp.maximum(best, pltpu.roll(best, 128 - 16, 1))
    total = jnp.where(sub < par_ref[16:17, :], best, 0.0)
    total = jnp.sum(total, axis=0, keepdims=True)
    out_ref[4, :, 0:128] = jnp.broadcast_to(total, (8, 128))
    out_ref[4, :, 128:256] = jnp.zeros((8, 128), jnp.float32)


def scan(par, xs, items):
    rows, width = xs[0].shape
    count = len(xs) * len(items)
    return pl.pallas_call(
        scan_kernel,
        in_specs=[IN_VMEM] * (1 + len(xs) + len(items)),
        out_specs=IN_VMEM,
        out_shape=jax.ShapeDtypeStruct((5, 8, rows), jnp.float32),
        scratch_shapes=[pltpu.VMEM((rows, 128), jnp.float32)],
        compiler_params=LARGE,
        cost_estimate=pl.CostEstimate(
            flops=2 * count * rows * rows * width,
            bytes_accessed=2 * (len(xs) + len(items)) * rows * width,
            transcendentals=0,
        ),
        name="scan",
    )(par, *xs, *items)


def score_kernel(par_ref, own_ref, over_ref, out_ref, wide_ref):
    rows = own_ref.shape[2]
    lane = lax.broadcasted_iota(jnp.int32, (8, rows), 1)
    lane128 = lax.broadcasted_iota(jnp.int32, (8, 128), 1)
    sub128 = lax.broadcasted_iota(jnp.int32, (8, 128), 0)
    par = par_ref[0:8]
    x_len = par[:, X_LEN : X_LEN + 1].astype(jnp.float32)
    sums = []
    for k in range(4):
        col = jnp.maximum(own_ref[k], over_ref[k ^ 2])
        valid = lane < par[:, A_VALID + k : A_VALID + k + 1]
        sums.append(jnp.sum(jnp.where(valid, col, 0.0), axis=1, keepdims=True))
    precision = own_ref[4][:, :128] + over_ref[4][:, :128]
    tile = jnp.zeros((8, 128), jnp.float32)
    for p in range(2):
        a_len = par[:, A_LEN + p : A_LEN + p + 1].astype(jnp.float32)
        recall = (sums[p] + sums[p + 2]) / a_len
        mine = jnp.where(lane128 == 8 * p + sub128, precision, 0.0)
        mine = jnp.sum(mine, axis=1, keepdims=True) / x_len
        tile = jnp.where(lane128 == p, 0.5 * (mine + recall), tile)
    out_ref[...] = tile
    wide_ref[0:8] = tile
    wide_ref[8:] = jnp.zeros((WIDE - 8, 128), jnp.float32)


def score(par, own, over):
    return pl.pallas_call(
        score_kernel,
        in_specs=[IN_VMEM] * 3,
        out_specs=[IN_VMEM] * 2,
        out_shape=[
            jax.ShapeDtypeStruct((8, 128), jnp.float32),
            jax.ShapeDtypeStruct((WIDE, 128), jnp.float32),
        ],
        compiler_params=SMALL,
        name="score",
    )(par, own, over)


def put_kernel(par_ref, own_ref, same_ref, other_ref, one_ref, two_ref, out_ref):
    y_lo, core = par_ref[0:1, Y_LO : Y_LO + 1], par_ref[0:1, CORE : CORE + 1]
    sub = lax.broadcasted_iota(jnp.int32, (16, 128), 0)
    lane = lax.broadcasted_iota(jnp.int32, (16, 128), 1)
    f, d, e = sub // 8, (sub % 8) // 2, sub % 2
    own = 2 * y_lo + core

    def add(total, values, steps, base, used):
        n = values.shape[0]
        use = used & (steps >= 1) & (steps <= STEPS) & (lane[:n] == base + steps - 1)
        return total + jnp.where(use, values, 0.0)

    part = jnp.zeros((8, 128), jnp.float32)
    for p, ref in enumerate((same_ref, other_ref)):
        values = ref[0:8, p : p + 1]
        x = 2 * (y_lo ^ p) + (core ^ e[:8])
        steps = GROUP * d[:8] + own - x
        part = add(part, values, steps, STEPS, steps == steps)
        part = add(part, values, -steps, 0, d[:8] == 0)
    total = jnp.zeros((16, 128), jnp.float32)
    for dist, ref in enumerate((own_ref, one_ref, two_ref), 1):
        for p in range(2):
            values = ref[:, p : p + 1]
            a = 2 * (y_lo ^ p) + (core ^ f)
            total = add(total, values, GROUP * dist + a - own, 0, (d == dist) & (e == f))
    total = jnp.sum(total, axis=0, keepdims=True) + jnp.sum(part, axis=0, keepdims=True)
    out_ref[...] = total[:, : 2 * STEPS]


def put(par, own, same, other, one, two):
    return pl.pallas_call(
        put_kernel,
        in_specs=[IN_VMEM] * 6,
        out_specs=IN_VMEM,
        out_shape=jax.ShapeDtypeStruct((1, 2 * STEPS), jnp.float32),
        compiler_params=SMALL,
        name="put",
    )(par, own, same, other, one, two)


def on_device(embeddings, lengths):
    device = lax.axis_index("cand")
    rows = embeddings.shape[1]
    ids = jnp.stack(
        [device // 4, (device // 2) % 2, device % 2, lax.axis_index("tok")]
    ).astype(jnp.int32)
    par = plan(ids, lengths, rows)
    own = normalize(embeddings)

    left = send(own, shift(dg=1))
    right = send(own, shift(dg=-1))
    over = send(own, shift(dh=1))
    own_c = send(own, shift(dc=1))
    left, own_c, par = lax.optimization_barrier((left, own_c, par))
    far = send(left, shift(dg=1))
    item1 = send(right, ring(1))
    item3 = send(right, ring(-1))
    left2, right2, over = lax.optimization_barrier((left, right, over))
    pair_c = send(jnp.concatenate([left2, right2]), shift(dc=1))
    over, right = lax.optimization_barrier((over, right))
    item2 = send(over, shift(dg=-1))
    far_c = send(far, shift(dc=1))
    left_c, right_c = pair_c, pair_c
    xs = [right, right_c, own, own_c, left, left_c, far, far_c]
    message = scan(par, xs, [right, item1, item2, item3])

    tile, wide = score(par, message, send(message, shift(dh=1)))
    other = send(wide, shift(dg=1, dl=1))
    same = send(wide, shift(dg=1))
    tiles = jnp.concatenate([tile, send(tile, shift(dc=1))])
    one = send(tiles, shift(dg=-1))
    two = send(tiles, shift(dg=-2))
    return put(par, tiles, same, other, one, two)


def solution(mesh):
    in_specs = (P("cand", "tok", None), P())
    out_specs = P("cand", None)
    return jax.shard_map(
        on_device, mesh=mesh, in_specs=in_specs, out_specs=out_specs, check_vma=False
    )
```

```python
import functools

import jax
import jax.numpy as jnp
from jax import lax
from jax.experimental import pallas as pl
from jax.experimental.pallas import tpu as pltpu
from jax.sharding import PartitionSpec as P

STEPS = 12
WIDE = 64
AXES = ("cand", "tok")
GROUP = 4
LOW = -4.0
SMALL = pltpu.CompilerParams(vmem_limit_bytes=4 * 1024 * 1024)
LARGE = pltpu.CompilerParams(vmem_limit_bytes=8 * 1024 * 1024)
IN_VMEM = pl.BlockSpec(memory_space=pltpu.VMEM)
IN_SMEM = pl.BlockSpec(memory_space=pltpu.SMEM)
X_VALID, X_LEN, A_VALID, A_LEN, Y_LO, CORE = 0, 1, 8, 16, 24, 25


def place(flat):
    return flat // 8, (flat // 4) % 2, (flat // 2) % 2, flat % 2


def flat(group, y_lo, core, y_hi, groups):
    return (((group % groups) * 2 + y_lo) * 2 + core) * 2 + y_hi


def send(value, move):
    count = lax.axis_size(AXES)
    groups = count // 8
    pairs = [(i, flat(*move(*place(i)), groups)) for i in range(count)]
    return lax.ppermute(value, AXES, pairs)


def shift(dg=0, dl=0, dc=0, dh=0):
    return lambda g, l, c, h: (g + dg, l ^ dl, c ^ dc, h ^ dh)


def ring(way):
    def move(g, l, c, h):
        y = (2 * h + l + (way if c == 0 else -way)) % 4
        return (g, y % 2, c, y // 2)

    return move


PARTS = 4


def normalize_kernel(emb_ref, out_ref):
    step = out_ref.shape[0] // PARTS
    for i in range(PARTS):
        values = emb_ref[i * step : (i + 1) * step, :].astype(jnp.float32)
        factor = lax.rsqrt(jnp.sum(values * values, axis=-1, keepdims=True) + 1e-06)
        out_ref[i * step : (i + 1) * step, :] = (values * factor).astype(jnp.bfloat16)


def normalize(emb):
    rows, width = emb.shape
    return pl.pallas_call(
        normalize_kernel,
        in_specs=[IN_VMEM],
        out_specs=IN_VMEM,
        out_shape=jax.ShapeDtypeStruct((rows, width), jnp.bfloat16),
        compiler_params=SMALL,
        name="normalize",
    )(emb)


def plan_kernel(rows, ids_ref, len_ref, par_ref):
    group, y_lo, core, y_hi = (ids_ref[i] for i in range(4))
    cands = len_ref.shape[0]
    sub = lax.broadcasted_iota(jnp.int32, (8, 128), 0)
    lane = lax.broadcasted_iota(jnp.int32, (8, 128), 1)
    for f in range(2):
        side = core ^ f
        tile = jnp.zeros((8, 128), jnp.int32)
        for x in range(8):
            cand = GROUP * (group + 1 - x // 2) + 2 * y_lo + (side ^ (x % 2))
            length = len_ref[(cand + cands) % cands]
            tile = jnp.where((sub == x) & (lane == X_VALID), length - rows * y_hi, tile)
            tile = jnp.where((sub == x) & (lane == X_LEN), length, tile)
        for k in range(4):
            y = (2 * y_hi + y_lo + jnp.where(side == 0, 4 - k, k)) % 4
            length = len_ref[(GROUP * (group + 1) + 2 * (y % 2) + side) % cands]
            tile = jnp.where(lane == A_VALID + k, length - rows * (y // 2), tile)
            if k < 2:
                tile = jnp.where(lane == A_LEN + k, length, tile)
        tile = jnp.where(lane == Y_LO, y_lo, tile)
        tile = jnp.where(lane == CORE, side, tile)
        par_ref[8 * f : 8 * f + 8] = tile
        if f == 0:
            turned = jnp.zeros((8, 128), jnp.int32)
            for x in range(8):
                cand = GROUP * (group + 1 - x // 2) + 2 * y_lo + (core ^ (x % 2))
                length = len_ref[(cand + cands) % cands]
                turned = jnp.where(lane % 8 == x, length - rows * y_hi, turned)
            par_ref[16:24] = turned


def plan(ids, lengths, rows):
    return pl.pallas_call(
        functools.partial(plan_kernel, rows),
        in_specs=[IN_SMEM] * 2,
        out_specs=IN_VMEM,
        out_shape=jax.ShapeDtypeStruct((24, 128), jnp.int32),
        compiler_params=SMALL,
        name="plan",
    )(ids, lengths)


def scan_kernel(par_ref, *refs):
    xs, items, out_ref, best_ref = refs[:8], refs[8:12], refs[12], refs[13]
    rows = xs[0].shape[0]
    lane = lax.broadcasted_iota(jnp.int32, (1, rows), 1)
    sub = lax.broadcasted_iota(jnp.int32, (rows, 1), 0)
    lane128 = lax.broadcasted_iota(jnp.int32, (1, 128), 1)
    best_ref[...] = jnp.full(best_ref.shape, LOW, jnp.float32)
    for k in (0, 1, 3, 2):
        a_mask = lane < par_ref[0:1, A_VALID + k : A_VALID + k + 1]
        for x in range(8):
            if x == 0 and k % 2 == 0:
                out_ref[k, x : x + 1, :] = jnp.full((1, rows), LOW, jnp.float32)
                continue
            x_mask = sub < par_ref[x : x + 1, X_VALID : X_VALID + 1]
            at = slice(rows, 2 * rows) if x == 1 else slice(0, rows)
            sims = lax.dot_general(
                xs[x][at, :],
                items[k][...],
                (((1,), (1,)), ((), ())),
                preferred_element_type=jnp.float32,
            )
            best = jnp.max(jnp.where(a_mask, sims, LOW), axis=1, keepdims=True)
            best_ref[...] = jnp.where(lane128 == 8 * k + x, best, best_ref[...])
            col = jnp.max(jnp.where(x_mask, sims, LOW), axis=0, keepdims=True)
            out_ref[k, x : x + 1, :] = col
    best = best_ref[...]
    best = jnp.maximum(best, pltpu.roll(best, 128 - 16, 1))
    total = jnp.where(sub < par_ref[16:17, :], best, 0.0)
    total = jnp.sum(total, axis=0, keepdims=True)
    out_ref[4, :, 0:128] = jnp.broadcast_to(total, (8, 128))
    out_ref[4, :, 128:256] = jnp.zeros((8, 128), jnp.float32)


def scan(par, xs, items):
    rows, width = xs[0].shape
    count = len(xs) * len(items)
    return pl.pallas_call(
        scan_kernel,
        in_specs=[IN_VMEM] * (1 + len(xs) + len(items)),
        out_specs=IN_VMEM,
        out_shape=jax.ShapeDtypeStruct((5, 8, rows), jnp.float32),
        scratch_shapes=[pltpu.VMEM((rows, 128), jnp.float32)],
        compiler_params=LARGE,
        cost_estimate=pl.CostEstimate(
            flops=2 * count * rows * rows * width,
            bytes_accessed=2 * (len(xs) + len(items)) * rows * width,
            transcendentals=0,
        ),
        name="scan",
    )(par, *xs, *items)


def score_kernel(par_ref, own_ref, over_ref, out_ref, wide_ref):
    rows = own_ref.shape[2]
    lane = lax.broadcasted_iota(jnp.int32, (8, rows), 1)
    lane128 = lax.broadcasted_iota(jnp.int32, (8, 128), 1)
    sub128 = lax.broadcasted_iota(jnp.int32, (8, 128), 0)
    par = par_ref[0:8]
    x_len = par[:, X_LEN : X_LEN + 1].astype(jnp.float32)
    sums = []
    for k in range(4):
        col = jnp.maximum(own_ref[k], over_ref[k ^ 2])
        valid = lane < par[:, A_VALID + k : A_VALID + k + 1]
        sums.append(jnp.sum(jnp.where(valid, col, 0.0), axis=1, keepdims=True))
    precision = own_ref[4][:, :128] + over_ref[4][:, :128]
    tile = jnp.zeros((8, 128), jnp.float32)
    for p in range(2):
        a_len = par[:, A_LEN + p : A_LEN + p + 1].astype(jnp.float32)
        recall = (sums[p] + sums[p + 2]) / a_len
        mine = jnp.where(lane128 == 8 * p + sub128, precision, 0.0)
        mine = jnp.sum(mine, axis=1, keepdims=True) / x_len
        tile = jnp.where(lane128 == p, 0.5 * (mine + recall), tile)
    out_ref[...] = tile
    wide_ref[0:8] = tile
    wide_ref[8:] = jnp.zeros((WIDE - 8, 128), jnp.float32)


def score(par, own, over):
    return pl.pallas_call(
        score_kernel,
        in_specs=[IN_VMEM] * 3,
        out_specs=[IN_VMEM] * 2,
        out_shape=[
            jax.ShapeDtypeStruct((8, 128), jnp.float32),
            jax.ShapeDtypeStruct((WIDE, 128), jnp.float32),
        ],
        compiler_params=SMALL,
        name="score",
    )(par, own, over)


def put_kernel(par_ref, own_ref, same_ref, other_ref, one_ref, two_ref, out_ref):
    y_lo, core = par_ref[0:1, Y_LO : Y_LO + 1], par_ref[0:1, CORE : CORE + 1]
    sub = lax.broadcasted_iota(jnp.int32, (16, 128), 0)
    lane = lax.broadcasted_iota(jnp.int32, (16, 128), 1)
    f, d, e = sub // 8, (sub % 8) // 2, sub % 2
    own = 2 * y_lo + core

    def add(total, values, steps, base, used):
        n = values.shape[0]
        use = used & (steps >= 1) & (steps <= STEPS) & (lane[:n] == base + steps - 1)
        return total + jnp.where(use, values, 0.0)

    part = jnp.zeros((8, 128), jnp.float32)
    for p, ref in enumerate((same_ref, other_ref)):
        values = ref[0:8, p : p + 1]
        x = 2 * (y_lo ^ p) + (core ^ e[:8])
        steps = GROUP * d[:8] + own - x
        part = add(part, values, steps, STEPS, steps == steps)
        part = add(part, values, -steps, 0, d[:8] == 0)
    total = jnp.zeros((16, 128), jnp.float32)
    for dist, ref in enumerate((own_ref, one_ref, two_ref), 1):
        for p in range(2):
            values = ref[:, p : p + 1]
            a = 2 * (y_lo ^ p) + (core ^ f)
            total = add(total, values, GROUP * dist + a - own, 0, (d == dist) & (e == f))
    total = jnp.sum(total, axis=0, keepdims=True) + jnp.sum(part, axis=0, keepdims=True)
    out_ref[...] = total[:, : 2 * STEPS]


def put(par, own, same, other, one, two):
    return pl.pallas_call(
        put_kernel,
        in_specs=[IN_VMEM] * 6,
        out_specs=IN_VMEM,
        out_shape=jax.ShapeDtypeStruct((1, 2 * STEPS), jnp.float32),
        compiler_params=SMALL,
        name="put",
    )(par, own, same, other, one, two)


def on_device(embeddings, lengths):
    device = lax.axis_index("cand")
    rows = embeddings.shape[1]
    ids = jnp.stack(
        [device // 4, (device // 2) % 2, device % 2, lax.axis_index("tok")]
    ).astype(jnp.int32)
    par = plan(ids, lengths, rows)
    raw = embeddings[0]
    left_raw = send(raw, shift(dg=1))
    right = normalize(send(raw, shift(dg=-1)))
    over = send(raw, shift(dh=1))
    own = normalize(raw)
    own_c = send(own, shift(dc=1))
    left_raw, par = lax.optimization_barrier((left_raw, par))
    far = normalize(send(left_raw, shift(dg=1)))
    left = normalize(left_raw)
    item1 = send(right, ring(1))
    item3 = send(right, ring(-1))
    left2, right2, over = lax.optimization_barrier((left, right, over))
    pair_c = send(jnp.concatenate([left2, right2]), shift(dc=1))
    over, right, own_c = lax.optimization_barrier((over, right, own_c))
    item2 = normalize(send(over, shift(dg=-1)))
    far_c = send(far, shift(dc=1))
    left_c, right_c = pair_c, pair_c
    xs = [right, right_c, own, own_c, left, left_c, far, far_c]
    message = scan(par, xs, [right, item1, item2, item3])

    tile, wide = score(par, message, send(message, shift(dh=1)))
    other = send(wide, shift(dg=1, dl=1))
    same = send(wide, shift(dg=1))
    tiles = jnp.concatenate([tile, send(tile, shift(dc=1))])
    one = send(tiles, shift(dg=-1))
    two = send(tiles, shift(dg=-2))
    return put(par, tiles, same, other, one, two)


def solution(mesh):
    in_specs = (P("cand", "tok", None), P())
    out_specs = P("cand", None)
    return jax.shard_map(
        on_device, mesh=mesh, in_specs=in_specs, out_specs=out_specs, check_vma=False
    )
```

```python
import functools

import jax
import jax.numpy as jnp
from jax import lax
from jax.experimental import pallas as pl
from jax.experimental.pallas import tpu as pltpu
from jax.sharding import PartitionSpec as P

STEPS = 12
WIDE = 24
AXES = ("cand", "tok")
GROUP = 4
LOW = -4.0
SMALL = pltpu.CompilerParams(vmem_limit_bytes=4 * 1024 * 1024)
LARGE = pltpu.CompilerParams(vmem_limit_bytes=8 * 1024 * 1024)
IN_VMEM = pl.BlockSpec(memory_space=pltpu.VMEM)
IN_SMEM = pl.BlockSpec(memory_space=pltpu.SMEM)
X_VALID, X_LEN, A_VALID, A_LEN, Y_LO, CORE = 0, 1, 8, 16, 24, 25


def place(flat):
    return flat // 8, (flat // 4) % 2, (flat // 2) % 2, flat % 2


def flat(group, y_lo, core, y_hi, groups):
    return (((group % groups) * 2 + y_lo) * 2 + core) * 2 + y_hi


def send(value, move):
    count = lax.axis_size(AXES)
    groups = count // 8
    pairs = [(i, flat(*move(*place(i)), groups)) for i in range(count)]
    return lax.ppermute(value, AXES, pairs)


def shift(dg=0, dl=0, dc=0, dh=0):
    return lambda g, l, c, h: (g + dg, l ^ dl, c ^ dc, h ^ dh)


def ring(way):
    def move(g, l, c, h):
        y = (2 * h + l + (way if c == 0 else -way)) % 4
        return (g, y % 2, c, y // 2)

    return move


PARTS = 4


def normalize_kernel(emb_ref, out_ref):
    step = out_ref.shape[0] // PARTS
    for i in range(PARTS):
        values = emb_ref[i * step : (i + 1) * step, :].astype(jnp.float32)
        factor = lax.rsqrt(jnp.sum(values * values, axis=-1, keepdims=True) + 1e-06)
        out_ref[i * step : (i + 1) * step, :] = (values * factor).astype(jnp.bfloat16)


def normalize(emb):
    rows, width = emb.shape
    return pl.pallas_call(
        normalize_kernel,
        in_specs=[IN_VMEM],
        out_specs=IN_VMEM,
        out_shape=jax.ShapeDtypeStruct((rows, width), jnp.bfloat16),
        compiler_params=SMALL,
        name="normalize",
    )(emb)


def plan_kernel(rows, ids_ref, len_ref, par_ref):
    group, y_lo, core, y_hi = (ids_ref[i] for i in range(4))
    cands = len_ref.shape[0]
    sub = lax.broadcasted_iota(jnp.int32, (8, 128), 0)
    lane = lax.broadcasted_iota(jnp.int32, (8, 128), 1)
    for f in range(2):
        side = core ^ f
        tile = jnp.zeros((8, 128), jnp.int32)
        for x in range(8):
            cand = GROUP * (group + 1 - x // 2) + 2 * y_lo + (side ^ (x % 2))
            length = len_ref[(cand + cands) % cands]
            tile = jnp.where((sub == x) & (lane == X_VALID), length - rows * y_hi, tile)
            tile = jnp.where((sub == x) & (lane == X_LEN), length, tile)
        for k in range(4):
            y = (2 * y_hi + y_lo + jnp.where(side == 0, 4 - k, k)) % 4
            length = len_ref[(GROUP * (group + 1) + 2 * (y % 2) + side) % cands]
            tile = jnp.where(lane == A_VALID + k, length - rows * (y // 2), tile)
            if k < 2:
                tile = jnp.where(lane == A_LEN + k, length, tile)
        tile = jnp.where(lane == Y_LO, y_lo, tile)
        tile = jnp.where(lane == CORE, side, tile)
        par_ref[8 * f : 8 * f + 8] = tile
        if f == 0:
            turned = jnp.zeros((8, 128), jnp.int32)
            for x in range(8):
                cand = GROUP * (group + 1 - x // 2) + 2 * y_lo + (core ^ (x % 2))
                length = len_ref[(cand + cands) % cands]
                turned = jnp.where(lane % 8 == x, length - rows * y_hi, turned)
            par_ref[16:24] = turned


def plan(ids, lengths, rows):
    return pl.pallas_call(
        functools.partial(plan_kernel, rows),
        in_specs=[IN_SMEM] * 2,
        out_specs=IN_VMEM,
        out_shape=jax.ShapeDtypeStruct((24, 128), jnp.int32),
        compiler_params=SMALL,
        name="plan",
    )(ids, lengths)


def scan_kernel(par_ref, *refs):
    xs, items, out_ref, best_ref = refs[:8], refs[8:12], refs[12], refs[13]
    rows = xs[0].shape[0]
    lane = lax.broadcasted_iota(jnp.int32, (1, rows), 1)
    sub = lax.broadcasted_iota(jnp.int32, (rows, 1), 0)
    lane128 = lax.broadcasted_iota(jnp.int32, (1, 128), 1)
    best_ref[...] = jnp.full(best_ref.shape, LOW, jnp.float32)
    for k in (0, 1, 3, 2):
        a_mask = lane < par_ref[0:1, A_VALID + k : A_VALID + k + 1]
        held = best_ref[...]
        for x in range(8):
            if x == 0 and k % 2 == 0:
                out_ref[k, x : x + 1, :] = jnp.full((1, rows), LOW, jnp.float32)
                continue
            x_mask = sub < par_ref[x : x + 1, X_VALID : X_VALID + 1]
            at = slice(rows, 2 * rows) if x == 1 else slice(0, rows)
            sims = lax.dot_general(
                xs[x][at, :],
                items[k][...],
                (((1,), (1,)), ((), ())),
                preferred_element_type=jnp.float32,
            )
            best = jnp.max(jnp.where(a_mask, sims, LOW), axis=1, keepdims=True)
            held = jnp.where(lane128 == 8 * k + x, best, held)
            col = jnp.max(jnp.where(x_mask, sims, LOW), axis=0, keepdims=True)
            out_ref[k, x : x + 1, :] = col
        best_ref[...] = held
    best = best_ref[...]
    best = jnp.maximum(best, pltpu.roll(best, 128 - 16, 1))
    total = jnp.where(sub < par_ref[16:17, :], best, 0.0)
    total = jnp.sum(total, axis=0, keepdims=True)
    out_ref[4, :, 0:128] = jnp.broadcast_to(total, (8, 128))
    out_ref[4, :, 128:256] = jnp.zeros((8, 128), jnp.float32)


def scan(par, xs, items):
    rows, width = xs[0].shape
    count = len(xs) * len(items)
    return pl.pallas_call(
        scan_kernel,
        in_specs=[IN_VMEM] * (1 + len(xs) + len(items)),
        out_specs=IN_VMEM,
        out_shape=jax.ShapeDtypeStruct((5, 8, rows), jnp.float32),
        scratch_shapes=[pltpu.VMEM((rows, 128), jnp.float32)],
        compiler_params=LARGE,
        cost_estimate=pl.CostEstimate(
            flops=2 * count * rows * rows * width,
            bytes_accessed=2 * (len(xs) + len(items)) * rows * width,
            transcendentals=0,
        ),
        name="scan",
    )(par, *xs, *items)


def score_kernel(par_ref, own_ref, over_ref, out_ref, wide_ref):
    rows = own_ref.shape[2]
    lane = lax.broadcasted_iota(jnp.int32, (8, rows), 1)
    lane128 = lax.broadcasted_iota(jnp.int32, (8, 128), 1)
    sub128 = lax.broadcasted_iota(jnp.int32, (8, 128), 0)
    par = par_ref[0:8]
    x_len = par[:, X_LEN : X_LEN + 1].astype(jnp.float32)
    sums = []
    for k in range(4):
        col = jnp.maximum(own_ref[k], over_ref[k ^ 2])
        valid = lane < par[:, A_VALID + k : A_VALID + k + 1]
        sums.append(jnp.sum(jnp.where(valid, col, 0.0), axis=1, keepdims=True))
    precision = own_ref[4][:, :128] + over_ref[4][:, :128]
    tile = jnp.zeros((8, 128), jnp.float32)
    for p in range(2):
        a_len = par[:, A_LEN + p : A_LEN + p + 1].astype(jnp.float32)
        recall = (sums[p] + sums[p + 2]) / a_len
        mine = jnp.where(lane128 == 8 * p + sub128, precision, 0.0)
        mine = jnp.sum(mine, axis=1, keepdims=True) / x_len
        tile = jnp.where(lane128 == p, 0.5 * (mine + recall), tile)
    out_ref[...] = tile
    wide_ref[0:8] = tile
    wide_ref[8:] = jnp.zeros((WIDE - 8, 128), jnp.float32)


def score(par, own, over):
    return pl.pallas_call(
        score_kernel,
        in_specs=[IN_VMEM] * 3,
        out_specs=[IN_VMEM] * 2,
        out_shape=[
            jax.ShapeDtypeStruct((8, 128), jnp.float32),
            jax.ShapeDtypeStruct((WIDE, 128), jnp.float32),
        ],
        compiler_params=SMALL,
        name="score",
    )(par, own, over)


def put_kernel(par_ref, own_ref, same_ref, other_ref, one_ref, two_ref, out_ref):
    y_lo, core = par_ref[0:1, Y_LO : Y_LO + 1], par_ref[0:1, CORE : CORE + 1]
    sub = lax.broadcasted_iota(jnp.int32, (16, 128), 0)
    lane = lax.broadcasted_iota(jnp.int32, (16, 128), 1)
    f, d, e = sub // 8, (sub % 8) // 2, sub % 2
    own = 2 * y_lo + core

    def add(total, values, steps, base, used):
        n = values.shape[0]
        use = used & (steps >= 1) & (steps <= STEPS) & (lane[:n] == base + steps - 1)
        return total + jnp.where(use, values, 0.0)

    part = jnp.zeros((8, 128), jnp.float32)
    for p, ref in enumerate((same_ref, other_ref)):
        values = ref[0:8, p : p + 1]
        x = 2 * (y_lo ^ p) + (core ^ e[:8])
        steps = GROUP * d[:8] + own - x
        part = add(part, values, steps, STEPS, steps == steps)
        part = add(part, values, -steps, 0, d[:8] == 0)
    total = jnp.zeros((16, 128), jnp.float32)
    for dist, ref in enumerate((own_ref, one_ref, two_ref), 1):
        for p in range(2):
            values = ref[:, p : p + 1]
            a = 2 * (y_lo ^ p) + (core ^ f)
            total = add(total, values, GROUP * dist + a - own, 0, (d == dist) & (e == f))
    total = jnp.sum(total, axis=0, keepdims=True) + jnp.sum(part, axis=0, keepdims=True)
    out_ref[...] = total[:, : 2 * STEPS]


def put(par, own, same, other, one, two):
    return pl.pallas_call(
        put_kernel,
        in_specs=[IN_VMEM] * 6,
        out_specs=IN_VMEM,
        out_shape=jax.ShapeDtypeStruct((1, 2 * STEPS), jnp.float32),
        compiler_params=SMALL,
        name="put",
    )(par, own, same, other, one, two)


def on_device(embeddings, lengths):
    device = lax.axis_index("cand")
    rows = embeddings.shape[1]
    ids = jnp.stack(
        [device // 4, (device // 2) % 2, device % 2, lax.axis_index("tok")]
    ).astype(jnp.int32)
    par = plan(ids, lengths, rows)
    raw = embeddings[0]
    left_raw = send(raw, shift(dg=1))
    right = normalize(send(raw, shift(dg=-1)))
    over = send(raw, shift(dh=1))
    own = normalize(raw)
    own_c = send(own, shift(dc=1))
    left_raw, par = lax.optimization_barrier((left_raw, par))
    far = normalize(send(left_raw, shift(dg=1)))
    left = normalize(left_raw)
    over, right, own_c = lax.optimization_barrier((over, right, own_c))
    item1 = send(right, ring(1))
    item3 = send(right, ring(-1))
    pair_c = send(jnp.concatenate([left, right]), shift(dc=1))
    item2 = normalize(send(over, shift(dg=-1)))
    far_c = send(far, shift(dc=1))
    left_c, right_c = pair_c, pair_c
    xs = [right, right_c, own, own_c, left, left_c, far, far_c]
    message = scan(par, xs, [right, item1, item2, item3])

    tile, wide = score(par, message, send(message, shift(dh=1)))
    other = send(wide, shift(dg=1, dl=1))
    same = send(wide, shift(dg=1))
    tiles = jnp.concatenate([tile, send(tile, shift(dc=1))])
    one = send(tiles, shift(dg=-1))
    two = send(tiles, shift(dg=-2))
    return put(par, tiles, same, other, one, two)


def solution(mesh):
    in_specs = (P("cand", "tok", None), P())
    out_specs = P("cand", None)
    return jax.shard_map(
        on_device, mesh=mesh, in_specs=in_specs, out_specs=out_specs, check_vma=False
    )
```

```python
import functools

import jax
import jax.numpy as jnp
from jax import lax
from jax.experimental import pallas as pl
from jax.experimental.pallas import tpu as pltpu
from jax.sharding import PartitionSpec as P

STEPS = 12
WIDE = 24
AXES = ("cand", "tok")
GROUP = 4
LOW = -4.0
SMALL = pltpu.CompilerParams(vmem_limit_bytes=4 * 1024 * 1024)
LARGE = pltpu.CompilerParams(vmem_limit_bytes=8 * 1024 * 1024)
IN_VMEM = pl.BlockSpec(memory_space=pltpu.VMEM)
IN_SMEM = pl.BlockSpec(memory_space=pltpu.SMEM)
X_VALID, X_LEN, A_VALID, A_LEN, Y_LO, CORE = 0, 1, 8, 16, 24, 25


def place(flat):
    return flat // 8, (flat // 4) % 2, (flat // 2) % 2, flat % 2


def flat(group, y_lo, core, y_hi, groups):
    return (((group % groups) * 2 + y_lo) * 2 + core) * 2 + y_hi


def send(value, move):
    count = lax.axis_size(AXES)
    groups = count // 8
    pairs = [(i, flat(*move(*place(i)), groups)) for i in range(count)]
    return lax.ppermute(value, AXES, pairs)


def shift(dg=0, dl=0, dc=0, dh=0):
    return lambda g, l, c, h: (g + dg, l ^ dl, c ^ dc, h ^ dh)


def ring(way):
    def move(g, l, c, h):
        y = (2 * h + l + (way if c == 0 else -way)) % 4
        return (g, y % 2, c, y // 2)

    return move


PARTS = 4


def normalize_kernel(emb_ref, out_ref):
    step = out_ref.shape[0] // PARTS
    for i in range(PARTS):
        values = emb_ref[i * step : (i + 1) * step, :].astype(jnp.float32)
        factor = lax.rsqrt(jnp.sum(values * values, axis=-1, keepdims=True) + 1e-06)
        out_ref[i * step : (i + 1) * step, :] = (values * factor).astype(jnp.bfloat16)


def normalize(emb):
    rows, width = emb.shape
    return pl.pallas_call(
        normalize_kernel,
        in_specs=[IN_VMEM],
        out_specs=IN_VMEM,
        out_shape=jax.ShapeDtypeStruct((rows, width), jnp.bfloat16),
        compiler_params=SMALL,
        name="normalize",
    )(emb)


def plan_kernel(rows, ids_ref, len_ref, par_ref):
    group, y_lo, core, y_hi = (ids_ref[i] for i in range(4))
    cands = len_ref.shape[0]
    sub = lax.broadcasted_iota(jnp.int32, (8, 128), 0)
    lane = lax.broadcasted_iota(jnp.int32, (8, 128), 1)
    for f in range(2):
        side = core ^ f
        tile = jnp.zeros((8, 128), jnp.int32)
        for x in range(8):
            cand = GROUP * (group + 1 - x // 2) + 2 * y_lo + (side ^ (x % 2))
            length = len_ref[(cand + cands) % cands]
            tile = jnp.where((sub == x) & (lane == X_VALID), length - rows * y_hi, tile)
            tile = jnp.where((sub == x) & (lane == X_LEN), length, tile)
        for k in range(4):
            y = (2 * y_hi + y_lo + jnp.where(side == 0, 4 - k, k)) % 4
            length = len_ref[(GROUP * (group + 1) + 2 * (y % 2) + side) % cands]
            tile = jnp.where(lane == A_VALID + k, length - rows * (y // 2), tile)
            if k < 2:
                tile = jnp.where(lane == A_LEN + k, length, tile)
        tile = jnp.where(lane == Y_LO, y_lo, tile)
        tile = jnp.where(lane == CORE, side, tile)
        par_ref[8 * f : 8 * f + 8] = tile
        if f == 0:
            turned = jnp.zeros((8, 128), jnp.int32)
            for x in range(8):
                cand = GROUP * (group + 1 - x // 2) + 2 * y_lo + (core ^ (x % 2))
                length = len_ref[(cand + cands) % cands]
                turned = jnp.where(lane % 8 == x, length - rows * y_hi, turned)
            par_ref[16:24] = turned


def plan(ids, lengths, rows):
    return pl.pallas_call(
        functools.partial(plan_kernel, rows),
        in_specs=[IN_SMEM] * 2,
        out_specs=IN_VMEM,
        out_shape=jax.ShapeDtypeStruct((24, 128), jnp.int32),
        compiler_params=SMALL,
        name="plan",
    )(ids, lengths)


def scan_kernel(par_ref, *refs):
    xs, items, out_ref, best_ref = refs[:8], refs[8:12], refs[12], refs[13]
    rows = xs[0].shape[0]
    lane = lax.broadcasted_iota(jnp.int32, (1, rows), 1)
    sub = lax.broadcasted_iota(jnp.int32, (rows, 1), 0)
    lane128 = lax.broadcasted_iota(jnp.int32, (1, 128), 1)
    best_ref[...] = jnp.full(best_ref.shape, LOW, jnp.float32)
    for k in (0, 1, 3, 2):
        a_mask = lane < par_ref[0:1, A_VALID + k : A_VALID + k + 1]
        held = best_ref[...]
        for x in range(8):
            if x == 0 and k % 2 == 0:
                out_ref[k, x : x + 1, :] = jnp.full((1, rows), LOW, jnp.float32)
                continue
            x_mask = sub < par_ref[x : x + 1, X_VALID : X_VALID + 1]
            at = slice(rows, 2 * rows) if x == 1 else slice(0, rows)
            sims = lax.dot_general(
                xs[x][at, :],
                items[k][...],
                (((1,), (1,)), ((), ())),
                preferred_element_type=jnp.float32,
            )
            best = jnp.max(jnp.where(a_mask, sims, LOW), axis=1, keepdims=True)
            held = jnp.where(lane128 == 8 * k + x, best, held)
            col = jnp.max(jnp.where(x_mask, sims, LOW), axis=0, keepdims=True)
            out_ref[k, x : x + 1, :] = col
        best_ref[...] = held
    best = best_ref[...]
    best = jnp.maximum(best, pltpu.roll(best, 128 - 16, 1))
    total = jnp.where(sub < par_ref[16:17, :], best, 0.0)
    total = jnp.sum(total, axis=0, keepdims=True)
    out_ref[4, :, 0:128] = jnp.broadcast_to(total, (8, 128))
    out_ref[4, :, 128:256] = jnp.zeros((8, 128), jnp.float32)


def scan(par, xs, items):
    rows, width = xs[0].shape
    count = len(xs) * len(items)
    return pl.pallas_call(
        scan_kernel,
        in_specs=[IN_VMEM] * (1 + len(xs) + len(items)),
        out_specs=IN_VMEM,
        out_shape=jax.ShapeDtypeStruct((5, 8, rows), jnp.float32),
        scratch_shapes=[pltpu.VMEM((rows, 128), jnp.float32)],
        compiler_params=LARGE,
        cost_estimate=pl.CostEstimate(
            flops=2 * count * rows * rows * width,
            bytes_accessed=2 * (len(xs) + len(items)) * rows * width,
            transcendentals=0,
        ),
        name="scan",
    )(par, *xs, *items)


def score_kernel(par_ref, own_ref, over_ref, out_ref, wide_ref):
    rows = own_ref.shape[2]
    lane = lax.broadcasted_iota(jnp.int32, (8, rows), 1)
    lane128 = lax.broadcasted_iota(jnp.int32, (8, 128), 1)
    sub128 = lax.broadcasted_iota(jnp.int32, (8, 128), 0)
    par = par_ref[0:8]
    x_len = par[:, X_LEN : X_LEN + 1].astype(jnp.float32)
    sums = []
    for k in range(4):
        col = jnp.maximum(own_ref[k], over_ref[k ^ 2])
        valid = lane < par[:, A_VALID + k : A_VALID + k + 1]
        sums.append(jnp.sum(jnp.where(valid, col, 0.0), axis=1, keepdims=True))
    precision = own_ref[4][:, :128] + over_ref[4][:, :128]
    tile = jnp.zeros((8, 128), jnp.float32)
    for p in range(2):
        a_len = par[:, A_LEN + p : A_LEN + p + 1].astype(jnp.float32)
        recall = (sums[p] + sums[p + 2]) / a_len
        mine = jnp.where(lane128 == 8 * p + sub128, precision, 0.0)
        mine = jnp.sum(mine, axis=1, keepdims=True) / x_len
        tile = jnp.where(lane128 == p, 0.5 * (mine + recall), tile)
    out_ref[...] = tile
    wide_ref[0:8] = tile
    wide_ref[8:] = jnp.zeros((WIDE - 8, 128), jnp.float32)


def score(par, own, over):
    return pl.pallas_call(
        score_kernel,
        in_specs=[IN_VMEM] * 3,
        out_specs=[IN_VMEM] * 2,
        out_shape=[
            jax.ShapeDtypeStruct((8, 128), jnp.float32),
            jax.ShapeDtypeStruct((WIDE, 128), jnp.float32),
        ],
        compiler_params=SMALL,
        name="score",
    )(par, own, over)


def put_kernel(par_ref, own_ref, same_ref, other_ref, one_ref, two_ref, out_ref):
    y_lo, core = par_ref[0:1, Y_LO : Y_LO + 1], par_ref[0:1, CORE : CORE + 1]
    sub = lax.broadcasted_iota(jnp.int32, (16, 128), 0)
    lane = lax.broadcasted_iota(jnp.int32, (16, 128), 1)
    f, d, e = sub // 8, (sub % 8) // 2, sub % 2
    own = 2 * y_lo + core

    def add(total, values, steps, base, used):
        n = values.shape[0]
        use = used & (steps >= 1) & (steps <= STEPS) & (lane[:n] == base + steps - 1)
        return total + jnp.where(use, values, 0.0)

    part = jnp.zeros((8, 128), jnp.float32)
    for p, ref in enumerate((same_ref, other_ref)):
        values = ref[0:8, p : p + 1]
        x = 2 * (y_lo ^ p) + (core ^ e[:8])
        steps = GROUP * d[:8] + own - x
        part = add(part, values, steps, STEPS, steps == steps)
        part = add(part, values, -steps, 0, d[:8] == 0)
    total = jnp.zeros((16, 128), jnp.float32)
    for dist, ref in enumerate((own_ref, one_ref, two_ref), 1):
        for p in range(2):
            values = ref[:, p : p + 1]
            a = 2 * (y_lo ^ p) + (core ^ f)
            total = add(total, values, GROUP * dist + a - own, 0, (d == dist) & (e == f))
    total = jnp.sum(total, axis=0, keepdims=True) + jnp.sum(part, axis=0, keepdims=True)
    out_ref[...] = total[:, : 2 * STEPS]


def put(par, own, same, other, one, two):
    return pl.pallas_call(
        put_kernel,
        in_specs=[IN_VMEM] * 6,
        out_specs=IN_VMEM,
        out_shape=jax.ShapeDtypeStruct((1, 2 * STEPS), jnp.float32),
        compiler_params=SMALL,
        name="put",
    )(par, own, same, other, one, two)


def on_device(embeddings, lengths):
    device = lax.axis_index("cand")
    rows = embeddings.shape[1]
    ids = jnp.stack(
        [device // 4, (device // 2) % 2, device % 2, lax.axis_index("tok")]
    ).astype(jnp.int32)
    par = plan(ids, lengths, rows)
    raw = embeddings[0]
    left_raw = send(raw, shift(dg=1))
    right = normalize(send(raw, shift(dg=-1)))
    over = send(raw, shift(dh=1))
    own = normalize(raw)
    own_c = send(own, shift(dc=1))
    left_raw, par = lax.optimization_barrier((left_raw, par))
    far = normalize(send(left_raw, shift(dg=1)))
    left_late, right = lax.optimization_barrier((left_raw, right))
    left = normalize(left_late)
    over, right, own_c = lax.optimization_barrier((over, right, own_c))
    item1 = send(right, ring(1))
    item3 = send(right, ring(-1))
    pair_c = send(jnp.concatenate([left, right]), shift(dc=1))
    item2 = normalize(send(over, shift(dg=-1)))
    far_c = send(far, shift(dc=1))
    left_c, right_c = pair_c, pair_c
    xs = [right, right_c, own, own_c, left, left_c, far, far_c]
    message = scan(par, xs, [right, item1, item2, item3])

    tile, wide = score(par, message, send(message, shift(dh=1)))
    other = send(wide, shift(dg=1, dl=1))
    same = send(wide, shift(dg=1))
    tiles = jnp.concatenate([tile, send(tile, shift(dc=1))])
    one = send(tiles, shift(dg=-1))
    two = send(tiles, shift(dg=-2))
    return put(par, tiles, same, other, one, two)


def solution(mesh):
    in_specs = (P("cand", "tok", None), P())
    out_specs = P("cand", None)
    return jax.shard_map(
        on_device, mesh=mesh, in_specs=in_specs, out_specs=out_specs, check_vma=False
    )
```
